32 devices in a mesh: req: 16 (over z, x, core), tp: 2 (over y).
Axes of the slice: x: 2, y: 2, z: 4, core: 2. Of those that a mesh axis runs over, the one named last changes fastest.
Arguments:
- gate_in: bfloat16 [2, 1024, 4096], P(None, 'req', 'tp'), may hold values from -6 to 6
- mix_in: bfloat16 [2, 1024, 4096], P(None, 'req', 'tp'), may hold values from -6 to 6
- keys_in: bfloat16 [2, 1024, 256], P(None, 'req'), may hold values from -6 to 6
- step_in: bfloat16 [2, 1024, 64], P(None, 'req', 'tp'), may hold values from -6 to 6
- resid_in: bfloat16 [2, 1024, 2048], P(None, 'req', 'tp'), may hold values from -12 to 12
- kernel_mix: float32 [2, 4, 4096], P(None, None, 'tp'), may hold values from -3 to 3
- kernel_keys: float32 [2, 4, 256], replicated, may hold values from -3 to 3
- step_bias: float32 [2, 64], P(None, 'tp'), may hold values from -4 to 0
- decay_rate: float32 [2, 64], P(None, 'tp'), may hold values from 0.02 to 2
- skip_gain: float32 [2, 64], P(None, 'tp'), may hold values from 0.5 to 1.5
- norm_gain: float32 [2, 4096], P(None, 'tp'), may hold values from 0.5 to 1.5
- final_gain: float32 [2, 2048], replicated, may hold values from 0.5 to 1.5
- out_weight: bfloat16 [2, 4096, 2048], P(None, 'tp', 'req'), may hold values from -0.09375 to 0.09375
- head_weight: bfloat16 [2, 25600, 2048], P(None, 'req'), may hold values from -8 to 8
- history_mix: bfloat16 [2, 48, 3, 4096], P(None, 'req', None, 'tp'), may hold values from -6 to 6
- history_keys: bfloat16 [2, 48, 3, 256], P(None, 'req'), may hold values from -6 to 6
- start_state: bfloat16 [2, 48, 4096, 128], P(None, 'req', 'tp'), may hold values from -0.59765625 to 0.59765625
- lengths: int32 [16, 3], P('req'), may hold values from 1 to 32, 64 in all within a row
- continued: int32 [16, 3], P('req'), may hold values 0 or 1
- targets: int32 [1024], P('req'), may hold values from 0 to 25599
- score_flag: int32 [1024], P('req'), may hold values 0 or 1
Outputs:
- logprobs: float32 [2, 1024], P(None, ('req', 'tp'))
The draws below stay inside these ranges and needn't reach their ends.
Inputs may be any that keep to these rules, and one draw needn't show every extreme that they name: The 3 lengths of a row fill its 64 slots exactly.
All inputs are finite; a program needn't handle non-finite values. No bound on the sum of `continued` or of `score_flag` on one device may be relied on, other than what follows from the above.
Results may differ from the reference program's by a relative error of at most 0.00075.
Values may be sent and summed in bfloat16 or wider, within the bound.
A program may use at most 128 MiB of HBM per device.

```python
import math
import jax
import jax.numpy as jnp
import numpy as np
from jax import lax

D = 2048
INNER = 4096
HEADS = 64
STATE = 128
VOCAB = 25600
CONV = 4
MODELS = 2
TOK_DEV = 64
REQ_DEV = 3
TOKENS = 1024
REQS = 48
N_REQ = 16


def common_signs(key):
    picks = jax.random.randint(jax.random.fold_in(key, 7), (D,), 0, 2)
    return jnp.where(picks == 1, 1.0, -1.0).astype(jnp.float32)


def draw_resid_in(key, part):
    signs = common_signs(key)
    base = jnp.clip(jax.random.normal(jax.random.fold_in(key, 1), (MODELS, TOKENS, D), jnp.float32), -6.0, 6.0)
    chosen = jax.random.randint(jax.random.fold_in(key, 2), (MODELS, TOKENS, 1), 0, 16) == 0
    aligned = 8.0 * signs[None, None, :] + 0.3 * base
    return jnp.where(chosen, aligned, base).astype(jnp.bfloat16)


def draw_head_weight(key, part):
    signs = common_signs(key)
    base = 0.07 * jnp.clip(jax.random.normal(jax.random.fold_in(key, 1), (MODELS, VOCAB, D), jnp.float32), -6.0, 6.0)
    level = 150.0
    stride = VOCAB // 8
    offset_row = jax.random.randint(jax.random.fold_in(key, 3), (), 0, stride)
    rows = jnp.arange(VOCAB, dtype=jnp.int32)
    strong = rows % stride == offset_row
    rank = (rows // stride).astype(jnp.float32)
    amplitude = (level + 2.0 * rank) / D
    aligned = amplitude[None, :, None] * signs[None, None, :] + 0.3 * base
    return jnp.where(strong[None, :, None], aligned, base).astype(jnp.bfloat16)


def place_ends(values, key, low, largest):
    spot = [jax.random.randint(jax.random.fold_in(key, axis), (), 0, length) for axis, length in enumerate(values.shape)]
    main_axis = values.shape.index(max(values.shape))
    neighbour = spot[:main_axis] + [(spot[main_axis] + 1) % values.shape[main_axis]] + spot[main_axis + 1:]
    return values.at[tuple(spot)].set(low).at[tuple(neighbour)].set(largest)


def steps_of(rng, dims, shards, low, high):
    loudness = 1.0
    for position, shards_of in shards:
        draws = jax.random.uniform(jax.random.fold_in(jax.random.fold_in(rng, 6), position), (shards_of,), jnp.float32, low / len(shards), high / len(shards))
        loudness = loudness * jnp.repeat(jnp.exp(draws), dims[position] // shards_of).reshape((-1,) + (1,) * (len(dims) - 1 - position))
    return loudness


def rank_table(number_of, skew):
    loads = [(1 << 20) // math.isqrt(grade ** skew) + 1 for grade in range(1, number_of + 1)]
    width = 1 + sum(loads) // (1 << 30)
    return np.cumsum(np.array([max(1, weight // width) for weight in loads]))


def ranked_ids(own_key, shape, count, slope):
    grid = rank_table(count, slope)
    ticket = jax.random.randint(jax.random.fold_in(own_key, 1), shape, 0, int(grid[count - 1]))
    rank = jnp.searchsorted(jnp.asarray(grid, jnp.int32), ticket, side="right")
    return jax.random.permutation(jax.random.fold_in(own_key, 2), count)[rank].astype(jnp.int32)


def split_up(count, total, most, lean):
    portions = [(1 << 20) // math.isqrt(grade ** lean) + 1 for grade in range(2, count + 1)]
    surplus, counts = total - most - (count - 1), [1] * (count - 1)
    while surplus > 0:
        movable = [i for i in range(count - 1) if counts[i] < most]
        whole, left = sum([portions[i] for i in movable]), surplus
        for i in movable:
            addition = min(most - counts[i], max(1, left * portions[i] // whole), surplus)
            counts[i] = counts[i] + addition
            surplus = surplus - addition
    return np.array([most] + counts)


def uneven(stream_key, amount, total, bound, lean):
    if amount == 2:
        one = jax.random.randint(stream_key, (), max(1, total - bound), min(bound, total - 1) + 1)
        return jnp.stack([one, total - one])
    sizes = jnp.asarray(split_up(amount, total, bound, lean), jnp.int32)
    pairs = (amount - 1) // 2
    source_of, taker = sizes[1:1 + 2 * pairs:2], sizes[2:2 + 2 * pairs:2]
    slack = jnp.minimum(source_of - 1, bound - taker)
    moved = jax.random.randint(jax.random.fold_in(stream_key, 1), (pairs,), 0, 1 << 20) % (slack + 1)
    sizes = sizes.at[1:1 + 2 * pairs:2].set(source_of - moved).at[2:2 + 2 * pairs:2].set(taker + moved)
    return sizes[jax.random.permutation(jax.random.fold_in(stream_key, 2), amount)]


def noise(key, dims, scale, most, shards=(), kind=jnp.bfloat16):
    entries = scale * jax.random.normal(key, dims, jnp.float32)
    if shards:
        entries = entries * steps_of(key, dims, shards, -0.22, 0.18)
    return jnp.clip(entries, -most, most).astype(kind)


def setup_inputs(seed: int = 0) -> dict:
    streams_of = jax.random.split(jax.random.key(seed), 22)
    gate_in = noise(streams_of[0], (MODELS, TOKENS, INNER), 1.0, 6.0, ((1, 16), (2, 2)))
    mix_in = noise(streams_of[1], (MODELS, TOKENS, INNER), 1.0, 6.0, ((1, 16), (2, 2)))
    keys_in = noise(streams_of[2], (MODELS, TOKENS, 2 * STATE), 1.0, 6.0, ((1, 16),))
    step_in = noise(streams_of[3], (MODELS, TOKENS, HEADS), 1.0, 6.0, ((1, 16), (2, 2)))
    resid_in = draw_resid_in(jax.random.fold_in(streams_of[21], 71), 0)
    kernel_mix = noise(streams_of[5], (MODELS, CONV, INNER), CONV ** -0.5, 3.0, ((2, 2),), jnp.float32)
    kernel_keys = noise(streams_of[6], (MODELS, CONV, 2 * STATE), CONV ** -0.5, 3.0, (), jnp.float32)
    step_bias = jnp.clip(-4.0 + 4.0 * jax.random.uniform(streams_of[7], (MODELS, HEADS), jnp.float32) ** steps_of(streams_of[7], (MODELS, HEADS), ((1, 2),), -0.2, 0.2), -4.0, 0.0)
    decay_rate = jnp.clip(jnp.exp(math.log(2.0) - 4.6051702 * jax.random.uniform(streams_of[8], (MODELS, HEADS), jnp.float32) ** steps_of(streams_of[8], (MODELS, HEADS), ((1, 2),), -0.2, 0.2)), 0.02, 2.0)
    skip_gain = jnp.clip(0.5 + 1.0 * jax.random.uniform(streams_of[9], (MODELS, HEADS), jnp.float32) ** steps_of(streams_of[9], (MODELS, HEADS), ((1, 2),), -0.2, 0.2), 0.5, 1.5)
    norm_gain = jnp.clip(1.0 + 0.1 * jax.random.normal(streams_of[10], (MODELS, INNER), jnp.float32), 0.5, 1.5)
    final_gain = jnp.clip(1.0 + 0.1 * jax.random.normal(streams_of[11], (MODELS, D), jnp.float32), 0.5, 1.5)
    out_weight = noise(streams_of[12], (MODELS, INNER, D), INNER ** -0.5, 0.09375, ((1, 2), (2, 16)))
    head_weight = draw_head_weight(jax.random.fold_in(streams_of[21], 71), 0)
    history_mix = noise(streams_of[14], (MODELS, REQS, CONV - 1, INNER), 1.0, 6.0, ((1, 16), (3, 2)))
    history_keys = noise(streams_of[15], (MODELS, REQS, CONV - 1, 2 * STATE), 1.0, 6.0, ((1, 16),))
    start_state = noise(streams_of[16], (MODELS, REQS, INNER, STATE), 0.1, 0.59765625, ((1, 16), (2, 2)))
    lengths = jax.vmap(lambda own: uneven(own, REQ_DEV, TOK_DEV, TOK_DEV // 2, 2))(jax.random.split(streams_of[17], N_REQ)).reshape((N_REQ, REQ_DEV)).astype(jnp.int32)
    continued = place_ends((jax.random.randint(streams_of[18], (N_REQ, REQ_DEV), 0, 2) < 1).astype(jnp.int32), jax.random.fold_in(streams_of[18], 1), 0, 1)
    targets = place_ends(ranked_ids(streams_of[19], (TOKENS,), VOCAB, 2), jax.random.fold_in(streams_of[19], 3), 0, VOCAB - 1).astype(jnp.int32)
    score_flag = place_ends((jax.random.randint(streams_of[20], (TOKENS,), 0, 4) < 3).astype(jnp.int32), jax.random.fold_in(streams_of[20], 1), 0, 1)
    return {"gate_in": gate_in, "mix_in": mix_in, "keys_in": keys_in, "step_in": step_in, "resid_in": resid_in, "kernel_mix": kernel_mix, "kernel_keys": kernel_keys, "step_bias": step_bias, "decay_rate": decay_rate, "skip_gain": skip_gain, "norm_gain": norm_gain, "final_gain": final_gain, "out_weight": out_weight, "head_weight": head_weight, "history_mix": history_mix, "history_keys": history_keys, "start_state": start_state, "lengths": lengths, "continued": continued, "targets": targets, "score_flag": score_flag}


EPSILON = 1e-05
PRECISE = lax.Precision.HIGHEST

def request_layout(lengths, step_count):
    lengths = lengths.astype(jnp.int32)
    starts = (jnp.cumsum(lengths) - lengths).astype(jnp.int32)
    time_index = jnp.arange(step_count, dtype=jnp.int32)
    segment = lax.optimization_barrier(jnp.sum((time_index[:, None] >= starts[None, 1:]).astype(jnp.int32), axis=1)).astype(jnp.int32)
    member = segment[:, None] == jnp.arange(lengths.shape[0], dtype=jnp.int32)[None, :]
    first_step = lax.optimization_barrier(jnp.sum(jnp.where(member, starts[None, :], 0), axis=1)).astype(jnp.int32)
    return (starts, segment, member, time_index - first_step)

def causal_conv(stream, kernel, history, member, offset):
    tap_count = kernel.shape[0]
    history_len = tap_count - 1
    current = stream.astype(jnp.float32)
    member_bf = member.astype(jnp.bfloat16)
    slot_values = [jnp.dot(member_bf, history[:, slot_index, :], preferred_element_type=jnp.float32) for slot_index in range(history_len)]
    output = kernel[history_len][None, :] * current
    for lag_steps in range(1, tap_count):
        shifted = jnp.concatenate([jnp.zeros((lag_steps, current.shape[1]), current.dtype), current[:-lag_steps]], axis=0)
        earlier = jnp.zeros_like(current)
        for slot_index in range(history_len):
            earlier = earlier + jnp.where((offset - lag_steps == slot_index - history_len)[:, None], slot_values[slot_index], 0.0)
        output = output + kernel[history_len - lag_steps][None, :] * jnp.where((offset >= lag_steps)[:, None], shifted, earlier)
    return jax.nn.silu(output)

def mixer_block(gate_rows, mix_rows, keys_rows, step_raw, kernel_mix, kernel_keys, step_bias, decay_rate, skip_gain, history_mix, history_keys, start_state, lengths, continued):
    step_count = gate_rows.shape[0]
    head_count = step_raw.shape[1]
    inner_width = mix_rows.shape[1]
    head_size = inner_width // head_count
    states = start_state.shape[2]
    starts, segment, member, offset = request_layout(lengths, step_count)
    keep_state = continued.astype(jnp.bfloat16)
    mixed = causal_conv(mix_rows, kernel_mix, history_mix * keep_state[:, None, None], member, offset)
    projected = causal_conv(keys_rows, kernel_keys, history_keys * keep_state[:, None, None], member, offset)
    inject = projected[:, :states]
    readout = projected[:, states:]
    step_size = jax.nn.softplus(step_raw.astype(jnp.float32) + step_bias[None, :])
    log_decay = -step_size * decay_rate[None, :]
    running = jnp.cumsum(log_decay, axis=0)
    time_index = jnp.arange(step_count, dtype=jnp.int32)
    causal = (segment[:, None] == segment[None, :]) & (time_index[:, None] >= time_index[None, :])
    spread = jnp.minimum(running[:, None, :] - running[None, :, :], 0.0)
    transfer = jnp.where(causal[:, :, None], jnp.exp(spread), 0.0)
    intersection = jnp.dot(readout, inject.T, precision=PRECISE)
    kernel_full = transfer * intersection[:, :, None]
    values = mixed.reshape(step_count, head_count, head_size)
    output = jnp.einsum('tsh,shp->thp', kernel_full, step_size[:, :, None] * values, precision=PRECISE)
    before = jnp.take(running - log_decay, starts, axis=0)
    member_float = member.astype(jnp.float32)
    entry_level = jnp.dot(member_float, before, precision=PRECISE)
    carried = jnp.exp(jnp.minimum(running - entry_level, 0.0))
    initial = start_state.astype(jnp.float32) * keep_state.astype(jnp.float32)[:, None, None]
    readings = jnp.einsum('tn,rcn->trc', readout, initial, precision=PRECISE)
    chosen = lax.optimization_barrier(jnp.sum(member_float[:, :, None] * readings, axis=1)).reshape(step_count, head_count, head_size)
    output = output + carried[:, :, None] * chosen + skip_gain[None, :, None] * values
    return output.reshape(step_count, inner_width) * jax.nn.silu(gate_rows.astype(jnp.float32))

def reference(gate_in, mix_in, keys_in, step_in, resid_in, kernel_mix, kernel_keys, step_bias, decay_rate, skip_gain, norm_gain, final_gain, out_weight, head_weight, history_mix, history_keys, start_state, lengths, continued, targets, score_flag):

    def per_block(array):
        return jnp.swapaxes(array.reshape((MODELS, N_REQ, TOK_DEV) + array.shape[2:]), 0, 1)

    def per_request(array):
        return jnp.swapaxes(array.reshape((MODELS, N_REQ, REQ_DEV) + array.shape[2:]), 0, 1)

    def score_block(block_args):
        gate_rows, mix_rows, keys_rows, step_rows, resid_rows, length_row, continued_row, state_mix, state_keys, state_ssm, target_row, flag_row = block_args
        results = []
        for model_index in range(MODELS):
            gated = mixer_block(gate_rows[model_index], mix_rows[model_index], keys_rows[model_index], step_rows[model_index], kernel_mix[model_index], kernel_keys[model_index], step_bias[model_index], decay_rate[model_index], skip_gain[model_index], state_mix[model_index], state_keys[model_index], state_ssm[model_index], length_row, continued_row)
            squares = lax.optimization_barrier(jnp.sum(gated * gated, axis=1))
            normed = (gated * lax.rsqrt(squares / INNER + EPSILON)[:, None] * norm_gain[model_index][None, :]).astype(jnp.bfloat16)
            update = jnp.dot(normed, out_weight[model_index], preferred_element_type=jnp.float32)
            hidden = (resid_rows[model_index].astype(jnp.float32) + update).astype(jnp.bfloat16)
            hidden_float = hidden.astype(jnp.float32)
            final_squares = lax.optimization_barrier(jnp.sum(hidden_float * hidden_float, axis=1))
            final_rows = (hidden_float * lax.rsqrt(final_squares / D + EPSILON)[:, None] * final_gain[model_index][None, :]).astype(jnp.bfloat16)
            logits = jnp.dot(final_rows, head_weight[model_index].T, preferred_element_type=jnp.float32)
            peak_logit = lax.optimization_barrier(jnp.max(logits, axis=1))
            normalizer = peak_logit + jnp.log(lax.optimization_barrier(jnp.sum(jnp.exp(logits - peak_logit[:, None]), axis=1)))
            picked = jnp.take_along_axis(logits, target_row[:, None].astype(jnp.int32), axis=1)[:, 0]
            results.append((picked - normalizer) * flag_row.astype(jnp.float32))
        return jnp.stack(results)
    block_inputs = (per_block(gate_in), per_block(mix_in), per_block(keys_in), per_block(step_in), per_block(resid_in), lengths, continued, per_request(history_mix), per_request(history_keys), per_request(start_state), targets.reshape(N_REQ, TOK_DEV), score_flag.reshape(N_REQ, TOK_DEV))
    scored = lax.map(score_block, block_inputs)
    return jnp.swapaxes(scored, 0, 1).reshape(MODELS, TOKENS)
```

```python
import functools

import jax
import jax.numpy as jnp
from jax import lax
from jax.experimental import pallas as pl
from jax.experimental.pallas import tpu as pltpu
from jax.sharding import PartitionSpec as P

EPSILON = 1e-05
PRECISE = lax.Precision.HIGHEST
MESH = pl.DeviceIdType.MESH
LANES = 128
CORES = 2


def request_layout(lengths, step_count):
    starts = jnp.cumsum(lengths) - lengths
    time_index = jnp.arange(step_count, dtype=jnp.int32)
    segment = jnp.sum((time_index[:, None] >= starts[None, 1:]).astype(jnp.int32), axis=1)
    member = segment[:, None] == jnp.arange(lengths.shape[0], dtype=jnp.int32)[None, :]
    first_step = jnp.sum(jnp.where(member, starts[None, :], 0), axis=1)
    return (starts, segment, member, time_index - first_step)


def causal_conv(stream, kernel, history, member, offset):
    tap_count = kernel.shape[0]
    history_len = tap_count - 1
    current = stream.astype(jnp.float32)
    member_bf = member.astype(jnp.bfloat16)
    slot_values = [
        jnp.dot(member_bf, history[:, slot_index, :], preferred_element_type=jnp.float32)
        for slot_index in range(history_len)
    ]
    output = kernel[history_len][None, :] * current
    for lag_steps in range(1, tap_count):
        shifted = jnp.concatenate(
            [jnp.zeros((lag_steps, current.shape[1]), current.dtype), current[:-lag_steps]], axis=0
        )
        earlier = jnp.zeros_like(current)
        for slot_index in range(history_len):
            earlier = earlier + jnp.where(
                (offset - lag_steps == slot_index - history_len)[:, None],
                slot_values[slot_index],
                0.0,
            )
        output = output + kernel[history_len - lag_steps][None, :] * jnp.where(
            (offset >= lag_steps)[:, None], shifted, earlier
        )
    return jax.nn.silu(output)


def mixer_block(
    gate_rows,
    mix_rows,
    keys_rows,
    step_raw,
    kernel_mix,
    kernel_keys,
    step_bias,
    decay_rate,
    skip_gain,
    history_mix,
    history_keys,
    start_state,
    lengths,
    continued,
):
    step_count = gate_rows.shape[0]
    head_count = step_raw.shape[1]
    inner_width = mix_rows.shape[1]
    head_size = inner_width // head_count
    states = start_state.shape[2]
    starts, segment, member, offset = request_layout(lengths, step_count)
    keep_state = continued.astype(jnp.bfloat16)
    mixed = causal_conv(
        mix_rows, kernel_mix, history_mix * keep_state[:, None, None], member, offset
    )
    projected = causal_conv(
        keys_rows, kernel_keys, history_keys * keep_state[:, None, None], member, offset
    )
    inject = projected[:, :states]
    readout = projected[:, states:]
    step_size = jax.nn.softplus(step_raw.astype(jnp.float32) + step_bias[None, :])
    log_decay = -step_size * decay_rate[None, :]
    running = jnp.cumsum(log_decay, axis=0)
    time_index = jnp.arange(step_count, dtype=jnp.int32)
    causal = (segment[:, None] == segment[None, :]) & (time_index[:, None] >= time_index[None, :])
    spread = jnp.minimum(running[:, None, :] - running[None, :, :], 0.0)
    transfer = jnp.where(causal[:, :, None], jnp.exp(spread), 0.0)
    intersection = jnp.dot(readout, inject.T, precision=PRECISE)
    kernel_full = transfer * intersection[:, :, None]
    values = mixed.reshape(step_count, head_count, head_size)
    output = jnp.einsum(
        "tsh,shp->thp", kernel_full, step_size[:, :, None] * values, precision=PRECISE
    )
    before = jnp.take(running - log_decay, starts, axis=0)
    member_float = member.astype(jnp.float32)
    entry_level = jnp.dot(member_float, before, precision=PRECISE)
    carried = jnp.exp(jnp.minimum(running - entry_level, 0.0))
    initial = start_state.astype(jnp.float32) * keep_state.astype(jnp.float32)[:, None, None]
    readings = jnp.einsum("tn,rcn->trc", readout, initial, precision=PRECISE)
    chosen = jnp.sum(member_float[:, :, None] * readings, axis=1).reshape(
        step_count, head_count, head_size
    )
    output = output + carried[:, :, None] * chosen + skip_gain[None, :, None] * values
    return output.reshape(step_count, inner_width) * jax.nn.silu(gate_rows.astype(jnp.float32))


def split_shards(shards):
    chips = shards // CORES
    inner = 1
    while inner * inner * 4 <= chips:
        inner *= 2
    return chips // inner, inner


def flipped(index, mask):
    value, bit = index, 1
    while bit <= mask:
        if mask & bit:
            value = value + bit - 2 * bit * ((index // bit) % 2)
        bit *= 2
    return value


def score_kernel(
    outer,
    inner,
    groups,
    gated_ref,
    gain_ref,
    final_gain_ref,
    resid_ref,
    local_ids_ref,
    weight_ref,
    head_ref,
    result_ref,
    weight,
    head,
    squares,
    normed,
    part,
    landed,
    total,
    hidden,
    final,
    stats,
    stats_in,
    weight_sem,
    head_sem,
    square_send,
    square_recv,
    normed_send,
    normed_recv,
    part_send,
    part_recv,
    hidden_send,
    hidden_recv,
    stats_send,
    stats_recv,
):
    me = lax.axis_index("req")
    lane = lax.axis_index("tp")
    columns = inner * CORES
    shards = outer * columns
    row, column = me // columns, me % columns
    x, core = column // CORES, column % CORES
    models, inner_part = gain_ref.shape
    slots = gated_ref.shape[0] // models
    share = slots // groups
    width = resid_ref.shape[2]
    features = width * outer
    line_rows = outer * share
    pending = []

    def send(source, target, send_sem, recv_sem, device):
        copy = pltpu.make_async_remote_copy(
            src_ref=source,
            dst_ref=target,
            send_sem=send_sem,
            recv_sem=recv_sem,
            device_id=device,
            device_id_type=MESH,
        )
        copy.start()
        pending.append(copy)

    def landing(buffer, recv_sem):
        pltpu.make_async_copy(buffer, buffer, recv_sem).wait()

    barrier = pltpu.get_barrier_semaphore()
    for step in range(1, shards):
        pl.semaphore_signal(
            barrier,
            inc=1,
            device_id=(lax.rem(me + step, shards), lane),
            device_id_type=MESH,
        )
    for step in range(1, groups):
        pl.semaphore_signal(
            barrier,
            inc=1,
            device_id=(me, lax.rem(lane + step, groups)),
            device_id_type=MESH,
        )

    if len(weight_ref.shape) == 4:
        block = weight_ref.shape[3]
        loads = [
            pltpu.make_async_copy(
                weight_ref.at[index],
                weight.at[:, :, pl.ds(index * block, block)],
                weight_sem.at[index],
            )
            for index in range(columns)
        ]
    else:
        loads = [pltpu.make_async_copy(weight_ref, weight, weight_sem.at[0])]
    for load in loads:
        load.start()
    head_loads = [
        pltpu.make_async_copy(head_ref.at[model], head.at[model], head_sem.at[model])
        for model in range(models)
    ]
    for load in head_loads:
        load.start()

    with jax.named_scope("gated_norm"):
        for model in range(models):
            rows = pl.ds(model * slots, slots)
            values = gated_ref[rows, :]
            own = jnp.sum(values * values, axis=1, keepdims=True)
            squares[lane, rows, :] = jnp.broadcast_to(own, (slots, LANES))
        pl.semaphore_wait(barrier, shards - 1 + groups - 1)
        for step in range(1, groups):
            send(
                squares.at[lane],
                squares.at[lane],
                square_send.at[step],
                square_recv.at[lane],
                (me, lax.rem(lane + step, groups)),
            )
        for step in range(1, groups):
            other = lax.rem(lane + step, groups)
            landing(squares.at[other], square_recv.at[other])
        for model in range(models):
            rows = pl.ds(model * slots, slots)
            level = squares[0, rows, 0:1]
            for group in range(1, groups):
                level = level + squares[group, rows, 0:1]
            scale = lax.rsqrt(level / (inner_part * groups) + EPSILON)
            normed[row, rows, :] = (
                gated_ref[rows, :] * scale * gain_ref[model : model + 1, :]
            ).astype(jnp.bfloat16)

    with jax.named_scope("out_projection"):
        for mask in range(1, outer):
            send(
                normed.at[row],
                normed.at[row],
                normed_send.at[mask],
                normed_recv.at[row],
                (flipped(row, mask) * columns + column, lane),
            )
        for load in loads:
            load.wait()
        for mask in range(outer):
            line = flipped(row, mask)
            if mask:
                landing(normed.at[line], normed_recv.at[line])
            for model in range(models):
                rows = pl.ds(model * slots, slots)
                product = jnp.dot(
                    normed[line, rows, :], weight[model], preferred_element_type=jnp.float32
                ) + resid_ref[line, rows, :].astype(jnp.float32)
                for group in range(groups):
                    part[group, line, pl.ds(model * share, share), :] = product[
                        group * share : (group + 1) * share
                    ]
            for step in range(1, groups):
                other = lax.rem(lane + step, groups)
                send(
                    part.at[other, line],
                    landed.at[lane, line],
                    part_send.at[step, mask],
                    part_recv.at[lane, line],
                    (me, other),
                )
        for mask in range(outer):
            line = flipped(row, mask)
            summed = part[lane, line]
            for step in range(1, groups):
                other = lax.rem(lane + step, groups)
                landing(landed.at[other, line], part_recv.at[other, line])
                summed = summed + landed[other, line]
            for model in range(models):
                start = pl.multiple_of(model * line_rows + line * share, share)
                total[pl.ds(start, share), :] = summed[model * share : (model + 1) * share]
        hidden[row, column] = total[...].astype(jnp.bfloat16)

    def normalize(source):
        level = None
        for line in range(outer):
            values = hidden[line, source].astype(jnp.float32)
            own = jnp.sum(values * values, axis=1, keepdims=True)
            level = own if level is None else level + own
        scale = lax.rsqrt(level / features + EPSILON)
        start = pl.multiple_of(source * line_rows, line_rows)
        for line in range(outer):
            for model in range(models):
                rows = slice(model * line_rows, (model + 1) * line_rows)
                values = hidden[line, source, rows, :].astype(jnp.float32)
                spot = slice(line * width, (line + 1) * width)
                final[model, pl.ds(start, line_rows), spot] = (
                    values * scale[rows] * final_gain_ref[model : model + 1, spot]
                ).astype(jnp.bfloat16)

    with jax.named_scope("gather_features"):
        counter = iter(range(hidden_send.shape[0]))

        def pass_on(line, source, device):
            send(
                hidden.at[line, source],
                hidden.at[line, source],
                hidden_send.at[next(counter)],
                hidden_recv.at[line, source],
                (device, lane),
            )

        for mask in range(1, outer):
            pass_on(row, column, flipped(row, mask) * columns + column)
        sibling = 1 - core
        for mask in range(outer):
            line = flipped(row, mask)
            if mask:
                landing(hidden.at[line, column], hidden_recv.at[line, column])
            for side in range(1, inner):
                pass_on(line, column, row * columns + flipped(x, side) * CORES + core)
            pass_on(line, column, row * columns + x * CORES + sibling)
        normalize(column)
        for side in range(1, inner):
            source = flipped(x, side) * CORES + core
            for mask in range(outer):
                line = flipped(row, mask)
                landing(hidden.at[line, source], hidden_recv.at[line, source])
                pass_on(line, source, row * columns + x * CORES + sibling)
            normalize(source)
        for side in range(inner):
            source = flipped(x, side) * CORES + sibling
            for mask in range(outer):
                line = flipped(row, mask)
                landing(hidden.at[line, source], hidden_recv.at[line, source])
            normalize(source)

    with jax.named_scope("head"):
        entries = head_ref.shape[1]
        tile = max(size for size in range(16, 401, 16) if entries % size == 0)
        tokens = final.shape[1]
        stats[...] = jnp.zeros_like(stats)
        for model in range(models):
            head_loads[model].wait()

            def scan(index, state, model=model):
                peak, spread, picked = state
                start = pl.multiple_of(index * tile, tile)
                logits = lax.dot_general(
                    head[model, pl.ds(start, tile), :],
                    final[model],
                    (((1,), (1,)), ((), ())),
                    preferred_element_type=jnp.float32,
                )
                new_peak = jnp.maximum(peak, jnp.max(logits, axis=0, keepdims=True))
                spread = spread * jnp.exp(peak - new_peak) + jnp.sum(
                    jnp.exp(logits - new_peak), axis=0, keepdims=True
                )
                entry = lax.broadcasted_iota(jnp.int32, (tile, tokens), 0) + start
                picked = picked + jnp.sum(
                    jnp.where(entry == local_ids_ref[0:1, :], logits, 0.0), axis=0, keepdims=True
                )
                return new_peak, spread, picked

            zero = jnp.zeros((1, tokens), jnp.float32)
            found = lax.fori_loop(0, entries // tile, scan, (zero - jnp.inf, zero, zero))
            for kind in range(3):
                for index in range(tokens // LANES):
                    stats[index, pl.ds(3 * model + kind, 1), :] = found[kind][
                        :, index * LANES : (index + 1) * LANES
                    ]

    with jax.named_scope("merge"):

        def tile_of(shard):
            return (((shard % columns) * outer + shard // columns) * share) // LANES

        for step in range(1, shards):
            other = lax.rem(me + step, shards)
            send(
                stats.at[tile_of(other)],
                stats_in.at[me],
                stats_send.at[step],
                stats_recv.at[me],
                (other, lane),
            )
        stats_in[me] = stats[tile_of(me)]
        for step in range(1, shards):
            other = lax.rem(me + step, shards)
            landing(stats_in.at[other], stats_recv.at[other])
        for model in range(models):
            peaks = stats_in[:, 3 * model, :]
            peak = jnp.max(peaks, axis=0, keepdims=True)
            spread = jnp.sum(
                stats_in[:, 3 * model + 1, :] * jnp.exp(peaks - peak), axis=0, keepdims=True
            )
            picked = jnp.sum(stats_in[:, 3 * model + 2, :], axis=0, keepdims=True)
            result_ref[model : model + 1, :] = picked - (peak + jnp.log(spread))
    for copy in pending:
        copy.wait_send()


def local(
    gate_in,
    mix_in,
    keys_in,
    step_in,
    resid_in,
    kernel_mix,
    kernel_keys,
    step_bias,
    decay_rate,
    skip_gain,
    norm_gain,
    final_gain,
    out_weight,
    head_weight,
    history_mix,
    history_keys,
    start_state,
    lengths,
    continued,
    targets,
    score_flag,
):
    groups = lax.axis_size("tp")
    shards = lax.axis_size("req")
    lane_index = lax.axis_index("tp")
    shard_index = lax.axis_index("req")
    outer, inner = split_shards(shards)
    columns = inner * CORES
    models, step_count, inner_part = gate_in.shape
    share = step_count // groups
    features = final_gain.shape[1]
    width = features // outer
    vocab_part = head_weight.shape[1]
    tokens = shards * share
    row, column = shard_index // columns, shard_index % columns
    lines = [[z * columns + c for z in range(outer)] for c in range(columns)]
    planes = [[z * columns + c for c in range(columns)] for z in range(outer)]

    if out_weight.shape[2] % LANES == 0:
        weights = lax.all_gather(out_weight, "req", axis_index_groups=planes)
    else:
        weights = lax.all_gather(out_weight, "req", axis=2, tiled=True, axis_index_groups=planes)
    resid_line = lax.all_gather(resid_in, "req", axis_index_groups=lines)
    per_group = outer // groups
    resid_part = lax.dynamic_slice_in_dim(resid_line, (row % per_group) * width, width, 3)
    resid_part = jnp.where(row // per_group == lane_index, resid_part, 0).reshape(
        outer, models * step_count, width
    )
    every_target = lax.all_gather(targets, "req").reshape(outer, columns, groups, share)
    own_targets = lax.dynamic_index_in_dim(every_target, lane_index, 2, False)
    local_ids = jnp.swapaxes(own_targets, 0, 1).reshape(1, tokens) - shard_index * vocab_part

    gated = jnp.concatenate(
        [
            mixer_block(
                gate_in[model_index],
                mix_in[model_index],
                keys_in[model_index],
                step_in[model_index],
                kernel_mix[model_index],
                kernel_keys[model_index],
                step_bias[model_index],
                decay_rate[model_index],
                skip_gain[model_index],
                history_mix[model_index],
                history_keys[model_index],
                start_state[model_index],
                lengths[0],
                continued[0],
            )
            for model_index in range(models)
        ]
    )
    rows = models * step_count
    line_rows = outer * share
    sends = outer - 1 + outer * (inner - 1) + outer * inner
    dma = pltpu.SemaphoreType.DMA
    vmem = pl.BlockSpec(memory_space=pltpu.VMEM)
    anywhere = pl.BlockSpec(memory_space=pl.ANY)
    scores = pl.pallas_call(
        functools.partial(score_kernel, outer, inner, groups),
        out_shape=jax.ShapeDtypeStruct((models, LANES), jnp.float32),
        in_specs=[vmem] * 5 + [anywhere] * 2,
        out_specs=vmem,
        scratch_shapes=[
            pltpu.VMEM((models, inner_part, width), jnp.bfloat16),
            pltpu.VMEM((models, vocab_part, features), jnp.bfloat16),
            pltpu.VMEM((groups, rows, LANES), jnp.float32),
            pltpu.VMEM((outer, rows, inner_part), jnp.bfloat16),
            pltpu.VMEM((groups, outer, models * share, width), jnp.float32),
            pltpu.VMEM((groups, outer, models * share, width), jnp.float32),
            pltpu.VMEM((models * line_rows, width), jnp.float32),
            pltpu.VMEM((outer, columns, models * line_rows, width), jnp.bfloat16),
            pltpu.VMEM((models, tokens, features), jnp.bfloat16),
            pltpu.VMEM((tokens // LANES, 8, LANES), jnp.float32),
            pltpu.VMEM((shards, 8, LANES), jnp.float32),
            dma((columns,)),
            dma((models,)),
            dma((groups,)),
            dma((groups,)),
            dma((outer,)),
            dma((outer,)),
            dma((groups, outer)),
            dma((groups, outer)),
            dma((sends,)),
            dma((outer, columns)),
            dma((shards,)),
            dma((shards,)),
        ],
        compiler_params=pltpu.CompilerParams(
            collective_id=0, has_side_effects=True, vmem_limit_bytes=50 * 1024 * 1024
        ),
    )(gated, norm_gain, final_gain, resid_part, local_ids, weights, head_weight)
    spot = ((column * outer + row) * share) % LANES
    own_scores = lax.dynamic_slice_in_dim(scores, spot, share, 1)
    scored_rows = lax.dynamic_slice_in_dim(score_flag, lane_index * share, share, 0)
    return own_scores * scored_rows.astype(jnp.float32)[None, :]


def solution(mesh):
    placed = (
        P(None, "req", "tp"),
        P(None, "req", "tp"),
        P(None, "req", None),
        P(None, "req", "tp"),
        P(None, "req", "tp"),
        P(None, None, "tp"),
        P(),
        P(None, "tp"),
        P(None, "tp"),
        P(None, "tp"),
        P(None, "tp"),
        P(),
        P(None, "tp", "req"),
        P(None, "req", None),
        P(None, "req", None, "tp"),
        P(None, "req", None, None),
        P(None, "req", "tp", None),
        P("req", None),
        P("req", None),
        P("req"),
        P("req"),
    )
    return jax.shard_map(
        local, mesh=mesh, in_specs=placed, out_specs=P(None, ("req", "tp")), check_vma=False
    )
```

```python
import functools

import jax
import jax.numpy as jnp
from jax import lax
from jax.experimental import pallas as pl
from jax.experimental.pallas import tpu as pltpu
from jax.sharding import PartitionSpec as P

EPSILON = 1e-05
PRECISE = lax.Precision.HIGHEST
MESH = pl.DeviceIdType.MESH
LANES = 128
CORES = 2
CHUNK = 256


def halves(values):
    high = values.astype(jnp.bfloat16)
    return high, (values - high.astype(jnp.float32)).astype(jnp.bfloat16)


def dot_f32(left, right, contract=((1,), (0,))):
    return lax.dot_general(left, right, (contract, ((), ())), preferred_element_type=jnp.float32)


def request_place(lengths_ref, shape, axis):
    slot = lax.broadcasted_iota(jnp.int32, shape, axis)
    segment, first, start = jnp.zeros_like(slot), jnp.zeros_like(slot), 0
    for request in range(1, lengths_ref.shape[1]):
        start = start + lengths_ref[0, request - 1]
        later = slot >= start
        segment = segment + later.astype(jnp.int32)
        first = jnp.where(later, start, first)
    return segment, slot - first


def conv_silu(current, taps, history, requests, segment, offset):
    tap_count = len(taps)
    output = taps[tap_count - 1] * current
    for lag in range(1, tap_count):
        earlier = pltpu.roll(current, lag, 0)
        for request in range(requests):
            for begin in range(lag):
                chosen = (segment == request) & (offset == begin)
                earlier = jnp.where(chosen, history[request][begin - lag + tap_count - 1], earlier)
        output = output + taps[tap_count - 1 - lag] * earlier
    return jax.nn.silu(output)


def mixer(
    model,
    gate_ref,
    mix_ref,
    keys_ref,
    step_ref,
    kernel_mix_ref,
    kernel_keys_ref,
    step_bias_ref,
    decay_rate_ref,
    skip_ref,
    history_mix_ref,
    history_keys_ref,
    state_ref,
    lengths_ref,
    continued_ref,
    gated,
):
    slots, inner_part = mix_ref.shape[1:]
    heads = step_ref.shape[2]
    head_size = inner_part // heads
    requests, states = state_ref.shape[1], state_ref.shape[3]
    taps = kernel_mix_ref.shape[1]
    several = CHUNK // head_size

    def rows_of(history_ref, spot):
        return [
            [
                history_ref[model, pl.ds(request * (taps - 1) + slot, 1), spot]
                for slot in range(taps - 1)
            ]
            for request in range(requests)
        ]

    segment, offset = request_place(lengths_ref, (slots, CHUNK), 0)
    every = slice(None)
    wide = keys_ref.shape[2]
    key_segment, key_offset = request_place(lengths_ref, (slots, wide), 0)
    projected = conv_silu(
        keys_ref[model].astype(jnp.float32),
        [kernel_keys_ref[model, pl.ds(tap, 1), :] for tap in range(taps)],
        rows_of(history_keys_ref, every),
        requests,
        key_segment,
        key_offset,
    )
    inject, readout = projected[:, :states], projected[:, states:]
    intersection = lax.dot_general(
        readout,
        inject,
        (((1,), (1,)), ((), ())),
        precision=PRECISE,
        preferred_element_type=jnp.float32,
    )
    row_segment = segment[:, :states]
    by_request = []
    for request in range(requests):
        keep = continued_ref[0, request].astype(jnp.float32)
        part = jnp.where(row_segment == request, readout, 0.0) * keep
        by_request.append(jnp.concatenate(halves(part), axis=0))

    square = (slots, slots)
    to_segment, _ = request_place(lengths_ref, square, 0)
    from_segment, _ = request_place(lengths_ref, square, 1)
    to_slot = lax.broadcasted_iota(jnp.int32, square, 0)
    from_slot = lax.broadcasted_iota(jnp.int32, square, 1)
    causal = ((to_segment == from_segment) & (to_slot >= from_slot)).astype(jnp.float32)
    same = (to_slot == from_slot).astype(jnp.float32)

    raw = step_ref[model].astype(jnp.float32) + step_bias_ref[pl.ds(model, 1), :]
    step_size = jnp.maximum(raw, 0.0) + jnp.log1p(jnp.exp(-jnp.abs(raw)))
    log_decay = -step_size * decay_rate_ref[pl.ds(model, 1), :]
    running = jnp.dot(causal, log_decay, precision=PRECISE, preferred_element_type=jnp.float32)
    carried = jnp.exp(jnp.minimum(running, 0.0))
    per_head = jnp.concatenate([running, step_size, carried], axis=0)
    strength = jnp.concatenate([causal * intersection] * several, axis=1)
    causal_wide = jnp.concatenate([causal] * several, axis=1)
    same_wide = jnp.concatenate([same] * several, axis=1)
    block_shape = (several * slots, CHUNK)
    block_row = lax.broadcasted_iota(jnp.int32, block_shape, 0)
    block_lane = lax.broadcasted_iota(jnp.int32, block_shape, 1)
    own_block = jnp.zeros(block_shape, jnp.float32)
    for index in range(several):
        inside = (
            (block_row >= index * slots)
            & (block_row < (index + 1) * slots)
            & (block_lane >= index * head_size)
            & (block_lane < (index + 1) * head_size)
        )
        own_block = jnp.where(inside, 1.0, own_block)

    def chunk(index, _):
        start = pl.multiple_of(index * CHUNK, CHUNK)
        spot = pl.ds(start, CHUNK)
        mixed = conv_silu(
            mix_ref[model, :, spot].astype(jnp.float32),
            [kernel_mix_ref[model, pl.ds(tap, 1), spot] for tap in range(taps)],
            rows_of(history_mix_ref, spot),
            requests,
            segment,
            offset,
        )
        first_unit = lax.broadcasted_iota(jnp.int32, (heads, CHUNK), 0) * head_size
        unit = lax.broadcasted_iota(jnp.int32, (heads, CHUNK), 1) + start
        of_head = ((unit >= first_unit) & (unit < first_unit + head_size)).astype(jnp.float32)
        spread_out = jnp.dot(
            per_head, of_head, precision=PRECISE, preferred_element_type=jnp.float32
        )
        run_to = spread_out[:slots]
        step_wide = spread_out[slots : 2 * slots]
        carried_wide = spread_out[2 * slots :]
        run_from = jnp.sum(run_to * same_wide, axis=0, keepdims=True)
        decay = jnp.exp(jnp.minimum(run_to - run_from, 0.0) * causal_wide)
        attend_high, attend_low = halves(decay * strength)
        values = jnp.concatenate([step_wide * mixed] * several, axis=0) * own_block
        value_high, value_low = halves(values)
        output = (
            dot_f32(attend_high, value_high)
            + dot_f32(attend_high, value_low)
            + dot_f32(attend_low, value_high)
        )
        readings = None
        for request in range(requests):
            term = dot_f32(by_request[request], state_ref[model, request, spot, :], ((1,), (1,)))
            readings = term if readings is None else readings + term
        chosen = readings[:slots] + readings[slots:]
        output = output + carried_wide * chosen + skip_ref[pl.ds(model, 1), spot] * mixed
        gate = gate_ref[model, :, spot].astype(jnp.float32)
        gated[pl.ds(model * slots, slots), spot] = output * jax.nn.silu(gate)
        return 0

    lax.fori_loop(0, inner_part // CHUNK, chunk, 0)


def split_shards(shards):
    chips = shards // CORES
    inner = 1
    while inner * inner * 4 <= chips:
        inner *= 2
    return chips // inner, inner


def flipped(index, mask):
    value, bit = index, 1
    while bit <= mask:
        if mask & bit:
            value = value + bit - 2 * bit * ((index // bit) % 2)
        bit *= 2
    return value


def score_kernel(
    outer,
    inner,
    groups,
    gate_ref,
    mix_ref,
    keys_ref,
    step_ref,
    kernel_mix_ref,
    kernel_keys_ref,
    step_bias_ref,
    decay_rate_ref,
    skip_ref,
    history_mix_ref,
    history_keys_ref,
    gain_ref,
    final_gain_ref,
    resid_ref,
    target_ref,
    lengths_ref,
    continued_ref,
    state_ref,
    weight_ref,
    head_ref,
    result_ref,
    state,
    gated_ref,
    resid,
    targets_in,
    weight,
    head,
    squares,
    normed,
    part,
    landed,
    total,
    hidden,
    final,
    stats,
    stats_in,
    state_sem,
    resid_send,
    resid_recv,
    target_send,
    target_recv,
    weight_sem,
    weight_send,
    weight_recv,
    head_sem,
    square_send,
    square_recv,
    normed_send,
    normed_recv,
    part_send,
    part_recv,
    hidden_send,
    hidden_recv,
    stats_send,
    stats_recv,
):
    me = lax.axis_index("req")
    lane = lax.axis_index("tp")
    columns = inner * CORES
    shards = outer * columns
    row, column = me // columns, me % columns
    x, core = column // CORES, column % CORES
    models, inner_part = gain_ref.shape
    slots = gate_ref.shape[1]
    share = slots // groups
    width = resid.shape[3]
    per_group = outer // groups
    sibling = 1 - core
    features = width * outer
    line_rows = outer * share
    pending = []

    def send(source, target, send_sem, recv_sem, device):
        copy = pltpu.make_async_remote_copy(
            src_ref=source,
            dst_ref=target,
            send_sem=send_sem,
            recv_sem=recv_sem,
            device_id=device,
            device_id_type=MESH,
        )
        copy.start()
        pending.append(copy)

    def landing(buffer, recv_sem):
        pltpu.make_async_copy(buffer, buffer, recv_sem).wait()

    barrier = pltpu.get_barrier_semaphore()
    for step in range(1, shards):
        pl.semaphore_signal(
            barrier,
            inc=1,
            device_id=(lax.rem(me + step, shards), lane),
            device_id_type=MESH,
        )
    for step in range(1, groups):
        pl.semaphore_signal(
            barrier,
            inc=1,
            device_id=(me, lax.rem(lane + step, groups)),
            device_id_type=MESH,
        )

    state_load = pltpu.make_async_copy(state_ref, state, state_sem)
    state_load.start()
    block = weight_ref.shape[2]
    exchanged = block % LANES == 0

    def columns_of(source):
        return weight.at[:, :, pl.ds(pl.multiple_of(source * block, block), block)]

    weight_load = pltpu.make_async_copy(
        weight_ref, columns_of(column) if exchanged else weight, weight_sem
    )
    weight_load.start()
    head_loads = [
        pltpu.make_async_copy(head_ref.at[model], head.at[model], head_sem.at[model])
        for model in range(models)
    ]
    for load in head_loads:
        load.start()

    pl.semaphore_wait(barrier, shards - 1 + groups - 1)

    def resid_copy(index):
        return pltpu.make_async_remote_copy(
            src_ref=resid_ref.at[:, :, pl.ds(index * width, width)],
            dst_ref=resid.at[row],
            send_sem=resid_send.at[index],
            recv_sem=resid_recv.at[row],
            device_id=((lane * per_group + index) * columns + column, lane),
            device_id_type=MESH,
        )

    with jax.named_scope("early_sends"):
        if exchanged:
            for side in range(1, inner):
                send(
                    weight_ref,
                    columns_of(column),
                    weight_send.at[side],
                    weight_recv.at[column],
                    (row * columns + flipped(x, side) * CORES + core, lane),
                )
            send(
                weight_ref,
                columns_of(column),
                weight_send.at[0],
                weight_recv.at[column],
                (row * columns + x * CORES + sibling, lane),
            )
        for index in range(per_group):
            pl.when(lane * per_group + index != row)(lambda index=index: resid_copy(index).start())
        for step in range(1, shards):
            send(
                target_ref,
                targets_in.at[me],
                target_send.at[step],
                target_recv.at[me],
                (lax.rem(me + step, shards), lane),
            )
        targets_in[me] = target_ref[...]

    with jax.named_scope("mixer"):
        state_load.wait()
        for model in range(models):
            mixer(
                model,
                gate_ref,
                mix_ref,
                keys_ref,
                step_ref,
                kernel_mix_ref,
                kernel_keys_ref,
                step_bias_ref,
                decay_rate_ref,
                skip_ref,
                history_mix_ref,
                history_keys_ref,
                state,
                lengths_ref,
                continued_ref,
                gated_ref,
            )

    with jax.named_scope("gated_norm"):
        for model in range(models):
            rows = pl.ds(model * slots, slots)
            values = gated_ref[rows, :]
            own = jnp.sum(values * values, axis=1, keepdims=True)
            squares[lane, rows, :] = jnp.broadcast_to(own, (slots, LANES))
        for step in range(1, groups):
            send(
                squares.at[lane],
                squares.at[lane],
                square_send.at[step],
                square_recv.at[lane],
                (me, lax.rem(lane + step, groups)),
            )
        for step in range(1, groups):
            other = lax.rem(lane + step, groups)
            landing(squares.at[other], square_recv.at[other])
        for model in range(models):
            rows = pl.ds(model * slots, slots)
            level = squares[0, rows, 0:1]
            for group in range(1, groups):
                level = level + squares[group, rows, 0:1]
            scale = lax.rsqrt(level / (inner_part * groups) + EPSILON)
            normed[row, rows, :] = (
                gated_ref[rows, :] * scale * gain_ref[model : model + 1, :]
            ).astype(jnp.bfloat16)

    with jax.named_scope("out_projection"):
        for mask in range(1, outer):
            send(
                normed.at[row],
                normed.at[row],
                normed_send.at[mask],
                normed_recv.at[row],
                (flipped(row, mask) * columns + column, lane),
            )
        weight_load.wait()
        if exchanged:
            for side in range(1, inner):
                other = flipped(x, side) * CORES + core
                landing(columns_of(other), weight_recv.at[other])
                send(
                    columns_of(other),
                    columns_of(other),
                    weight_send.at[inner + side - 1],
                    weight_recv.at[other],
                    (row * columns + x * CORES + sibling, lane),
                )

        @pl.when(row // per_group == lane)
        def _():
            for index in range(per_group):

                @pl.when(lane * per_group + index == row)
                def _():
                    resid[row] = resid_ref[:, :, index * width : (index + 1) * width]

            for mask in range(1, outer):
                line = flipped(row, mask)
                landing(resid.at[line], resid_recv.at[line])

        @pl.when(row // per_group != lane)
        def _():
            resid[...] = jnp.zeros_like(resid)

        if exchanged:
            for side in range(inner):
                other = flipped(x, side) * CORES + sibling
                landing(columns_of(other), weight_recv.at[other])
        for mask in range(outer):
            line = flipped(row, mask)
            if mask:
                landing(normed.at[line], normed_recv.at[line])
            for model in range(models):
                rows = pl.ds(model * slots, slots)
                product = jnp.dot(
                    normed[line, rows, :], weight[model], preferred_element_type=jnp.float32
                ) + resid[line, model].astype(jnp.float32)
                for group in range(groups):
                    part[group, line, pl.ds(model * share, share), :] = product[
                        group * share : (group + 1) * share
                    ]
            for step in range(1, groups):
                other = lax.rem(lane + step, groups)
                send(
                    part.at[other, line],
                    landed.at[lane, line],
                    part_send.at[step, mask],
                    part_recv.at[lane, line],
                    (me, other),
                )
        for mask in range(outer):
            line = flipped(row, mask)
            summed = part[lane, line]
            for step in range(1, groups):
                other = lax.rem(lane + step, groups)
                landing(landed.at[other, line], part_recv.at[other, line])
                summed = summed + landed[other, line]
            for model in range(models):
                start = pl.multiple_of(model * line_rows + line * share, share)
                total[pl.ds(start, share), :] = summed[model * share : (model + 1) * share]
        hidden[row, column] = total[...].astype(jnp.bfloat16)

    def normalize(source):
        level = None
        for line in range(outer):
            values = hidden[line, source].astype(jnp.float32)
            own = jnp.sum(values * values, axis=1, keepdims=True)
            level = own if level is None else level + own
        scale = lax.rsqrt(level / features + EPSILON)
        start = pl.multiple_of(source * line_rows, line_rows)
        for line in range(outer):
            for model in range(models):
                rows = slice(model * line_rows, (model + 1) * line_rows)
                values = hidden[line, source, rows, :].astype(jnp.float32)
                spot = slice(line * width, (line + 1) * width)
                final[model, pl.ds(start, line_rows), spot] = (
                    values * scale[rows] * final_gain_ref[model : model + 1, spot]
                ).astype(jnp.bfloat16)

    with jax.named_scope("gather_features"):
        counter = iter(range(hidden_send.shape[0]))

        def pass_on(line, source, device):
            send(
                hidden.at[line, source],
                hidden.at[line, source],
                hidden_send.at[next(counter)],
                hidden_recv.at[line, source],
                (device, lane),
            )

        for mask in range(1, outer):
            pass_on(row, column, flipped(row, mask) * columns + column)
        for mask in range(outer):
            line = flipped(row, mask)
            if mask:
                landing(hidden.at[line, column], hidden_recv.at[line, column])
            for side in range(1, inner):
                pass_on(line, column, row * columns + flipped(x, side) * CORES + core)
            pass_on(line, column, row * columns + x * CORES + sibling)
        normalize(column)
        for side in range(1, inner):
            source = flipped(x, side) * CORES + core
            for mask in range(outer):
                line = flipped(row, mask)
                landing(hidden.at[line, source], hidden_recv.at[line, source])
                pass_on(line, source, row * columns + x * CORES + sibling)
            normalize(source)
        for side in range(inner):
            source = flipped(x, side) * CORES + sibling
            for mask in range(outer):
                line = flipped(row, mask)
                landing(hidden.at[line, source], hidden_recv.at[line, source])
            normalize(source)

    with jax.named_scope("head"):
        entries = head_ref.shape[1]
        tile = max(size for size in range(16, 401, 16) if entries % size == 0)
        tokens = final.shape[1]
        stats[...] = jnp.zeros_like(stats)
        for step in range(1, shards):
            other = lax.rem(me + step, shards)
            landing(targets_in.at[other], target_recv.at[other])
        tiles = [None] * (tokens // LANES)
        for source in range(columns):
            for line in range(outer):
                index = ((source * outer + line) * share) // LANES
                term = targets_in[line * columns + source, 0:1, :]
                tiles[index] = term if tiles[index] is None else tiles[index] + term
        local_ids = jnp.concatenate(tiles, axis=1) - me * entries
        for model in range(models):
            head_loads[model].wait()

            def scan(index, state, model=model):
                peak, spread, picked = state
                start = pl.multiple_of(index * tile, tile)
                logits = lax.dot_general(
                    head[model, pl.ds(start, tile), :],
                    final[model],
                    (((1,), (1,)), ((), ())),
                    preferred_element_type=jnp.float32,
                )
                new_peak = jnp.maximum(peak, jnp.max(logits, axis=0, keepdims=True))
                spread = spread * jnp.exp(peak - new_peak) + jnp.sum(
                    jnp.exp(logits - new_peak), axis=0, keepdims=True
                )
                entry = lax.broadcasted_iota(jnp.int32, (tile, tokens), 0) + start
                picked = picked + jnp.sum(
                    jnp.where(entry == local_ids, logits, 0.0), axis=0, keepdims=True
                )
                return new_peak, spread, picked

            zero = jnp.zeros((1, tokens), jnp.float32)
            found = lax.fori_loop(0, entries // tile, scan, (zero - jnp.inf, zero, zero))
            for kind in range(3):
                for index in range(tokens // LANES):
                    stats[index, pl.ds(3 * model + kind, 1), :] = found[kind][
                        :, index * LANES : (index + 1) * LANES
                    ]

    with jax.named_scope("merge"):

        def tile_of(shard):
            return (((shard % columns) * outer + shard // columns) * share) // LANES

        for step in range(1, shards):
            other = lax.rem(me + step, shards)
            send(
                stats.at[tile_of(other)],
                stats_in.at[me],
                stats_send.at[step],
                stats_recv.at[me],
                (other, lane),
            )
        stats_in[me] = stats[tile_of(me)]
        for step in range(1, shards):
            other = lax.rem(me + step, shards)
            landing(stats_in.at[other], stats_recv.at[other])
        for model in range(models):
            peaks = stats_in[:, 3 * model, :]
            peak = jnp.max(peaks, axis=0, keepdims=True)
            spread = jnp.sum(
                stats_in[:, 3 * model + 1, :] * jnp.exp(peaks - peak), axis=0, keepdims=True
            )
            picked = jnp.sum(stats_in[:, 3 * model + 2, :], axis=0, keepdims=True)
            result_ref[model : model + 1, :] = picked - (peak + jnp.log(spread))
    for index in range(per_group):
        pl.when(lane * per_group + index != row)(lambda index=index: resid_copy(index).wait_send())
    for copy in pending:
        copy.wait_send()


def local(
    gate_in,
    mix_in,
    keys_in,
    step_in,
    resid_in,
    kernel_mix,
    kernel_keys,
    step_bias,
    decay_rate,
    skip_gain,
    norm_gain,
    final_gain,
    out_weight,
    head_weight,
    history_mix,
    history_keys,
    start_state,
    lengths,
    continued,
    targets,
    score_flag,
):
    groups = lax.axis_size("tp")
    shards = lax.axis_size("req")
    lane_index = lax.axis_index("tp")
    shard_index = lax.axis_index("req")
    outer, inner = split_shards(shards)
    columns = inner * CORES
    models, step_count, inner_part = gate_in.shape
    share = step_count // groups
    features = final_gain.shape[1]
    width = features // outer
    vocab_part = head_weight.shape[1]
    tokens = shards * share
    row, column = shard_index // columns, shard_index % columns
    weights = out_weight
    if out_weight.shape[2] % LANES:
        planes = [[z * columns + c for c in range(columns)] for z in range(outer)]
        weights = lax.all_gather(out_weight, "req", axis=2, tiled=True, axis_index_groups=planes)
    spot = ((column * outer + row) * share) % LANES
    own_targets = lax.dynamic_slice_in_dim(targets, lane_index * share, share, 0)
    target_tile = jnp.broadcast_to(
        lax.dynamic_update_slice_in_dim(jnp.zeros(LANES, jnp.int32), own_targets, spot, 0)[None, :],
        (8, LANES),
    )
    skip_wide = jnp.repeat(skip_gain, inner_part // skip_gain.shape[1], axis=1)
    requests, past = history_mix.shape[1:3]
    history_rows = history_mix * continued[0].astype(jnp.bfloat16)[:, None, None]
    history_rows = history_rows.astype(jnp.float32).reshape(models, requests * past, inner_part)
    key_rows = history_keys * continued[0].astype(jnp.bfloat16)[:, None, None]
    key_rows = key_rows.astype(jnp.float32).reshape(models, requests * past, keys_in.shape[2])
    rows = models * step_count
    line_rows = outer * share
    sends = outer - 1 + outer * (inner - 1) + outer * inner
    dma = pltpu.SemaphoreType.DMA
    vmem = pl.BlockSpec(memory_space=pltpu.VMEM)
    smem = pl.BlockSpec(memory_space=pltpu.SMEM)
    anywhere = pl.BlockSpec(memory_space=pl.ANY)
    scores = pl.pallas_call(
        functools.partial(score_kernel, outer, inner, groups),
        out_shape=jax.ShapeDtypeStruct((models, LANES), jnp.float32),
        in_specs=[vmem] * 15 + [smem] * 2 + [anywhere] * 3,
        out_specs=vmem,
        scratch_shapes=[
            pltpu.VMEM(start_state.shape, jnp.bfloat16),
            pltpu.VMEM((rows, inner_part), jnp.float32),
            pltpu.VMEM((outer, models, step_count, width), jnp.bfloat16),
            pltpu.VMEM((shards, 8, LANES), jnp.int32),
            pltpu.VMEM((models, inner_part, width), jnp.bfloat16),
            pltpu.VMEM((models, vocab_part, features), jnp.bfloat16),
            pltpu.VMEM((groups, rows, LANES), jnp.float32),
            pltpu.VMEM((outer, rows, inner_part), jnp.bfloat16),
            pltpu.VMEM((groups, outer, models * share, width), jnp.float32),
            pltpu.VMEM((groups, outer, models * share, width), jnp.float32),
            pltpu.VMEM((models * line_rows, width), jnp.float32),
            pltpu.VMEM((outer, columns, models * line_rows, width), jnp.bfloat16),
            pltpu.VMEM((models, tokens, features), jnp.bfloat16),
            pltpu.VMEM((tokens // LANES, 8, LANES), jnp.float32),
            pltpu.VMEM((shards, 8, LANES), jnp.float32),
            dma,
            dma((outer // groups,)),
            dma((outer,)),
            dma((shards,)),
            dma((shards,)),
            dma,
            dma((2 * inner,)),
            dma((columns,)),
            dma((models,)),
            dma((groups,)),
            dma((groups,)),
            dma((outer,)),
            dma((outer,)),
            dma((groups, outer)),
            dma((groups, outer)),
            dma((sends,)),
            dma((outer, columns)),
            dma((shards,)),
            dma((shards,)),
        ],
        compiler_params=pltpu.CompilerParams(
            collective_id=0, has_side_effects=True, vmem_limit_bytes=50 * 1024 * 1024
        ),
    )(
        gate_in,
        mix_in,
        keys_in,
        step_in,
        kernel_mix,
        kernel_keys,
        step_bias,
        decay_rate,
        skip_wide,
        history_rows,
        key_rows,
        norm_gain,
        final_gain,
        resid_in,
        target_tile,
        lengths,
        continued,
        start_state,
        weights,
        head_weight,
    )
    own_scores = lax.dynamic_slice_in_dim(scores, spot, share, 1)
    scored_rows = lax.dynamic_slice_in_dim(score_flag, lane_index * share, share, 0)
    return own_scores * scored_rows.astype(jnp.float32)[None, :]


def solution(mesh):
    placed = (
        P(None, "req", "tp"),
        P(None, "req", "tp"),
        P(None, "req", None),
        P(None, "req", "tp"),
        P(None, "req", "tp"),
        P(None, None, "tp"),
        P(),
        P(None, "tp"),
        P(None, "tp"),
        P(None, "tp"),
        P(None, "tp"),
        P(),
        P(None, "tp", "req"),
        P(None, "req", None),
        P(None, "req", None, "tp"),
        P(None, "req", None, None),
        P(None, "req", "tp", None),
        P("req", None),
        P("req", None),
        P("req"),
        P("req"),
    )
    return jax.shard_map(
        local, mesh=mesh, in_specs=placed, out_specs=P(None, ("req", "tp")), check_vma=False
    )
```

```python
import functools

import jax
import jax.numpy as jnp
from jax import lax
from jax.experimental import pallas as pl
from jax.experimental.pallas import tpu as pltpu
from jax.sharding import PartitionSpec as P

EPSILON = 1e-05
PRECISE = lax.Precision.HIGHEST
MESH = pl.DeviceIdType.MESH
LANES = 128
CORES = 2
CHUNK = 256


def halves(values):
    high = values.astype(jnp.bfloat16)
    return high, (values - high.astype(jnp.float32)).astype(jnp.bfloat16)


def dot_f32(left, right, contract=((1,), (0,))):
    return lax.dot_general(left, right, (contract, ((), ())), preferred_element_type=jnp.float32)


def request_place(lengths_ref, shape, axis):
    slot = lax.broadcasted_iota(jnp.int32, shape, axis)
    segment, first, start = jnp.zeros_like(slot), jnp.zeros_like(slot), 0
    for request in range(1, lengths_ref.shape[1]):
        start = start + lengths_ref[0, request - 1]
        later = slot >= start
        segment = segment + later.astype(jnp.int32)
        first = jnp.where(later, start, first)
    return segment, slot - first


def conv_silu(current, taps, history, requests, segment, offset):
    tap_count = len(taps)
    output = taps[tap_count - 1] * current
    for lag in range(1, tap_count):
        earlier = pltpu.roll(current, lag, 0)
        for request in range(requests):
            for begin in range(lag):
                chosen = (segment == request) & (offset == begin)
                earlier = jnp.where(chosen, history[request][begin - lag + tap_count - 1], earlier)
        output = output + taps[tap_count - 1 - lag] * earlier
    return jax.nn.silu(output)


def mixer(
    model,
    gate_ref,
    mix_ref,
    keys_ref,
    step_ref,
    kernel_mix_ref,
    kernel_keys_ref,
    step_bias_ref,
    decay_rate_ref,
    skip_ref,
    history_mix_ref,
    history_keys_ref,
    state_ref,
    lengths_ref,
    continued_ref,
    gated,
):
    slots, inner_part = mix_ref.shape[1:]
    heads = step_ref.shape[2]
    head_size = inner_part // heads
    requests, states = state_ref.shape[1], state_ref.shape[3]
    taps = kernel_mix_ref.shape[1]
    several = CHUNK // head_size

    keeps = [continued_ref[0, request].astype(jnp.float32) for request in range(requests)]

    def rows_of(history_ref, spot):
        return [
            [
                history_ref[model, request, pl.ds(slot, 1), spot].astype(jnp.float32)
                * keeps[request]
                for slot in range(taps - 1)
            ]
            for request in range(requests)
        ]

    segment, offset = request_place(lengths_ref, (slots, CHUNK), 0)
    every = slice(None)
    wide = keys_ref.shape[2]
    key_segment, key_offset = request_place(lengths_ref, (slots, wide), 0)
    projected = conv_silu(
        keys_ref[model].astype(jnp.float32),
        [kernel_keys_ref[model, pl.ds(tap, 1), :] for tap in range(taps)],
        rows_of(history_keys_ref, every),
        requests,
        key_segment,
        key_offset,
    )
    inject, readout = projected[:, :states], projected[:, states:]
    intersection = lax.dot_general(
        readout,
        inject,
        (((1,), (1,)), ((), ())),
        precision=PRECISE,
        preferred_element_type=jnp.float32,
    )
    row_segment = segment[:, :states]
    by_request = []
    for request in range(requests):
        part = jnp.where(row_segment == request, readout, 0.0) * keeps[request]
        by_request.append(jnp.concatenate(halves(part), axis=0))

    square = (slots, slots)
    to_segment, _ = request_place(lengths_ref, square, 0)
    from_segment, _ = request_place(lengths_ref, square, 1)
    to_slot = lax.broadcasted_iota(jnp.int32, square, 0)
    from_slot = lax.broadcasted_iota(jnp.int32, square, 1)
    causal = ((to_segment == from_segment) & (to_slot >= from_slot)).astype(jnp.float32)
    same = (to_slot == from_slot).astype(jnp.float32)

    raw = step_ref[model].astype(jnp.float32) + step_bias_ref[pl.ds(model, 1), :]
    step_size = jnp.maximum(raw, 0.0) + jnp.log1p(jnp.exp(-jnp.abs(raw)))
    log_decay = -step_size * decay_rate_ref[pl.ds(model, 1), :]
    running = jnp.dot(causal, log_decay, precision=PRECISE, preferred_element_type=jnp.float32)
    carried = jnp.exp(jnp.minimum(running, 0.0))
    skip = jnp.broadcast_to(skip_ref[pl.ds(model, 1), :], (8, heads))
    per_head = jnp.concatenate([running, step_size, carried, skip], axis=0)
    strength = jnp.concatenate([causal * intersection] * several, axis=1)
    causal_wide = jnp.concatenate([causal] * several, axis=1)
    same_wide = jnp.concatenate([same] * several, axis=1)
    block_shape = (several * slots, CHUNK)
    block_row = lax.broadcasted_iota(jnp.int32, block_shape, 0)
    block_lane = lax.broadcasted_iota(jnp.int32, block_shape, 1)
    own_block = jnp.zeros(block_shape, jnp.float32)
    for index in range(several):
        inside = (
            (block_row >= index * slots)
            & (block_row < (index + 1) * slots)
            & (block_lane >= index * head_size)
            & (block_lane < (index + 1) * head_size)
        )
        own_block = jnp.where(inside, 1.0, own_block)

    def chunk(index, _):
        start = pl.multiple_of(index * CHUNK, CHUNK)
        spot = pl.ds(start, CHUNK)
        mixed = conv_silu(
            mix_ref[model, :, spot].astype(jnp.float32),
            [kernel_mix_ref[model, pl.ds(tap, 1), spot] for tap in range(taps)],
            rows_of(history_mix_ref, spot),
            requests,
            segment,
            offset,
        )
        first_unit = lax.broadcasted_iota(jnp.int32, (heads, CHUNK), 0) * head_size
        unit = lax.broadcasted_iota(jnp.int32, (heads, CHUNK), 1) + start
        of_head = ((unit >= first_unit) & (unit < first_unit + head_size)).astype(jnp.float32)
        spread_out = jnp.dot(
            per_head, of_head, precision=PRECISE, preferred_element_type=jnp.float32
        )
        run_to = spread_out[:slots]
        step_wide = spread_out[slots : 2 * slots]
        carried_wide = spread_out[2 * slots : 3 * slots]
        skip_wide = spread_out[3 * slots : 3 * slots + 1]
        run_from = jnp.sum(run_to * same_wide, axis=0, keepdims=True)
        decay = jnp.exp(jnp.minimum(run_to - run_from, 0.0) * causal_wide)
        attend_high, attend_low = halves(decay * strength)
        values = jnp.concatenate([step_wide * mixed] * several, axis=0) * own_block
        value_high, value_low = halves(values)
        output = (
            dot_f32(attend_high, value_high)
            + dot_f32(attend_high, value_low)
            + dot_f32(attend_low, value_high)
        )
        readings = None
        for request in range(requests):
            term = dot_f32(by_request[request], state_ref[model, request, spot, :], ((1,), (1,)))
            readings = term if readings is None else readings + term
        chosen = readings[:slots] + readings[slots:]
        output = output + carried_wide * chosen + skip_wide * mixed
        gate = gate_ref[model, :, spot].astype(jnp.float32)
        gated[pl.ds(model * slots, slots), spot] = output * jax.nn.silu(gate)
        return 0

    lax.fori_loop(0, inner_part // CHUNK, chunk, 0)


def split_shards(shards):
    chips = shards // CORES
    inner = 1
    while inner * inner * 4 <= chips:
        inner *= 2
    return chips // inner, inner


def flipped(index, mask):
    value, bit = index, 1
    while bit <= mask:
        if mask & bit:
            value = value + bit - 2 * bit * ((index // bit) % 2)
        bit *= 2
    return value


def score_kernel(outer, inner, groups, operand_count, *refs):
    operands, refs = refs[:operand_count], refs[operand_count:]
    lengths_ref, continued_ref, state_ref, weight_ref, head_ref, result_ref = refs[:6]
    copies, refs = refs[6 : 6 + operand_count], refs[6 + operand_count :]
    mixer_copies, (gain_ref, final_gain_ref, resid_ref, target_ref) = copies[:-4], copies[-4:]
    gate_ref = copies[0]
    (
        operand_sem,
        state,
        gated_ref,
        resid,
        targets_in,
        weight,
        head,
        squares,
        normed,
        part,
        landed,
        total,
        hidden,
        final,
        stats,
        stats_in,
        state_sem,
        resid_send,
        resid_recv,
        target_send,
        target_recv,
        weight_sem,
        weight_send,
        weight_recv,
        head_sem,
        square_send,
        square_recv,
        normed_send,
        normed_recv,
        part_send,
        part_recv,
        hidden_send,
        hidden_recv,
        stats_send,
        stats_recv,
    ) = refs
    me = lax.axis_index("req")
    lane = lax.axis_index("tp")
    columns = inner * CORES
    shards = outer * columns
    row, column = me // columns, me % columns
    x, core = column // CORES, column % CORES
    models, inner_part = gain_ref.shape
    slots = gate_ref.shape[1]
    share = slots // groups
    width = resid.shape[3]
    per_group = outer // groups
    sibling = 1 - core
    features = width * outer
    line_rows = outer * share
    pending = []

    def send(source, target, send_sem, recv_sem, device):
        copy = pltpu.make_async_remote_copy(
            src_ref=source,
            dst_ref=target,
            send_sem=send_sem,
            recv_sem=recv_sem,
            device_id=device,
            device_id_type=MESH,
        )
        copy.start()
        pending.append(copy)

    def landing(buffer, recv_sem):
        pltpu.make_async_copy(buffer, buffer, recv_sem).wait()

    loads = [
        pltpu.make_async_copy(operand, copy, operand_sem.at[index])
        for index, (operand, copy) in enumerate(zip(operands, copies))
    ]
    for load in loads:
        load.start()
    barrier = pltpu.get_barrier_semaphore()
    for step in range(1, shards):
        pl.semaphore_signal(
            barrier,
            inc=1,
            device_id=(lax.rem(me + step, shards), lane),
            device_id_type=MESH,
        )
    for step in range(1, groups):
        pl.semaphore_signal(
            barrier,
            inc=1,
            device_id=(me, lax.rem(lane + step, groups)),
            device_id_type=MESH,
        )

    state_load = pltpu.make_async_copy(state_ref, state, state_sem)
    state_load.start()
    block = weight_ref.shape[2]
    exchanged = block % LANES == 0

    def columns_of(source):
        return weight.at[:, :, pl.ds(pl.multiple_of(source * block, block), block)]

    weight_load = pltpu.make_async_copy(
        weight_ref, columns_of(column) if exchanged else weight, weight_sem
    )
    weight_load.start()
    head_loads = [
        pltpu.make_async_copy(head_ref.at[model], head.at[model], head_sem.at[model])
        for model in range(models)
    ]
    for load in head_loads:
        load.start()

    for load in loads:
        load.wait()
    pl.semaphore_wait(barrier, shards - 1 + groups - 1)

    def resid_copy(index):
        return pltpu.make_async_remote_copy(
            src_ref=resid_ref.at[:, :, pl.ds(index * width, width)],
            dst_ref=resid.at[row],
            send_sem=resid_send.at[index],
            recv_sem=resid_recv.at[row],
            device_id=((lane * per_group + index) * columns + column, lane),
            device_id_type=MESH,
        )

    with jax.named_scope("early_sends"):
        if exchanged:
            for side in range(1, inner):
                send(
                    weight_ref,
                    columns_of(column),
                    weight_send.at[side],
                    weight_recv.at[column],
                    (row * columns + flipped(x, side) * CORES + core, lane),
                )
            send(
                weight_ref,
                columns_of(column),
                weight_send.at[0],
                weight_recv.at[column],
                (row * columns + x * CORES + sibling, lane),
            )
        for index in range(per_group):
            pl.when(lane * per_group + index != row)(lambda index=index: resid_copy(index).start())
        for step in range(1, shards):
            send(
                target_ref,
                targets_in.at[me],
                target_send.at[step],
                target_recv.at[me],
                (lax.rem(me + step, shards), lane),
            )
        targets_in[me] = target_ref[...]

    def mix(model):
        with jax.named_scope("mixer"):
            mixer(model, *mixer_copies, state, lengths_ref, continued_ref, gated_ref)
            rows = pl.ds(model * slots, slots)
            values = gated_ref[rows, :]
            own = jnp.sum(values * values, axis=1, keepdims=True)
            squares[lane, model] = jnp.broadcast_to(own, (slots, LANES))
            for step in range(1, groups):
                send(
                    squares.at[lane, model],
                    squares.at[lane, model],
                    square_send.at[step, model],
                    square_recv.at[lane, model],
                    (me, lax.rem(lane + step, groups)),
                )

    def gated_norm(model):
        with jax.named_scope("gated_norm"):
            for step in range(1, groups):
                other = lax.rem(lane + step, groups)
                landing(squares.at[other, model], square_recv.at[other, model])
            rows = pl.ds(model * slots, slots)
            level = squares[0, model, :, 0:1]
            for group in range(1, groups):
                level = level + squares[group, model, :, 0:1]
            scale = lax.rsqrt(level / (inner_part * groups) + EPSILON)
            normed[model, row] = (
                gated_ref[rows, :] * scale * gain_ref[model : model + 1, :]
            ).astype(jnp.bfloat16)
            for mask in range(1, outer):
                send(
                    normed.at[model, row],
                    normed.at[model, row],
                    normed_send.at[model, mask],
                    normed_recv.at[model, row],
                    (flipped(row, mask) * columns + column, lane),
                )

    def pass_weights():
        weight_load.wait()
        if exchanged:
            for side in range(1, inner):
                other = flipped(x, side) * CORES + core
                landing(columns_of(other), weight_recv.at[other])
                send(
                    columns_of(other),
                    columns_of(other),
                    weight_send.at[inner + side - 1],
                    weight_recv.at[other],
                    (row * columns + x * CORES + sibling, lane),
                )

        @pl.when(row // per_group == lane)
        def _():
            for index in range(per_group):

                @pl.when(lane * per_group + index == row)
                def _():
                    resid[row] = resid_ref[:, :, index * width : (index + 1) * width]

            for mask in range(1, outer):
                line = flipped(row, mask)
                landing(resid.at[line], resid_recv.at[line])

        @pl.when(row // per_group != lane)
        def _():
            resid[...] = jnp.zeros_like(resid)

        if exchanged:
            for side in range(inner):
                other = flipped(x, side) * CORES + sibling
                landing(columns_of(other), weight_recv.at[other])

    def project(model):
        with jax.named_scope("out_projection"):
            for mask in range(outer):
                line = flipped(row, mask)
                if mask:
                    landing(normed.at[model, line], normed_recv.at[model, line])
                product = jnp.dot(
                    normed[model, line], weight[model], preferred_element_type=jnp.float32
                ) + resid[line, model].astype(jnp.float32)
                for group in range(groups):
                    part[group, model, line] = product[group * share : (group + 1) * share]
                for step in range(1, groups):
                    other = lax.rem(lane + step, groups)
                    send(
                        part.at[other, model, line],
                        landed.at[lane, model, line],
                        part_send.at[step, model, mask],
                        part_recv.at[lane, model, line],
                        (me, other),
                    )

    def pass_on(model, line, source, device):
        send(
            hidden.at[model, line, source],
            hidden.at[model, line, source],
            hidden_send.at[model, next(counters[model])],
            hidden_recv.at[model, line, source],
            (device, lane),
        )

    def reduce(model):
        with jax.named_scope("reduce_groups"):
            for mask in range(outer):
                line = flipped(row, mask)
                summed = part[lane, model, line]
                for step in range(1, groups):
                    other = lax.rem(lane + step, groups)
                    landing(landed.at[other, model, line], part_recv.at[other, model, line])
                    summed = summed + landed[other, model, line]
                total[pl.ds(pl.multiple_of(line * share, share), share), :] = summed
            hidden[model, row, column] = total[...].astype(jnp.bfloat16)
            for mask in range(1, outer):
                pass_on(model, row, column, flipped(row, mask) * columns + column)

    def normalize(model, source):
        level = None
        for line in range(outer):
            values = hidden[model, line, source].astype(jnp.float32)
            own = jnp.sum(values * values, axis=1, keepdims=True)
            level = own if level is None else level + own
        scale = lax.rsqrt(level / features + EPSILON)
        start = pl.multiple_of(source * line_rows, line_rows)
        for line in range(outer):
            values = hidden[model, line, source].astype(jnp.float32)
            spot = slice(line * width, (line + 1) * width)
            final[model, pl.ds(start, line_rows), spot] = (
                values * scale * final_gain_ref[model : model + 1, spot]
            ).astype(jnp.bfloat16)

    def arrived(model, line, source):
        landing(hidden.at[model, line, source], hidden_recv.at[model, line, source])

    def pass_line(model):
        for mask in range(outer):
            line = flipped(row, mask)
            if mask:
                arrived(model, line, column)
            for side in range(1, inner):
                pass_on(model, line, column, row * columns + flipped(x, side) * CORES + core)
            pass_on(model, line, column, row * columns + x * CORES + sibling)
        normalize(model, column)

    def pass_plane(model):
        for side in range(1, inner):
            source = flipped(x, side) * CORES + core
            for mask in range(outer):
                line = flipped(row, mask)
                arrived(model, line, source)
                pass_on(model, line, source, row * columns + x * CORES + sibling)
            normalize(model, source)

    def collect(model):
        for side in range(inner):
            source = flipped(x, side) * CORES + sibling
            for mask in range(outer):
                arrived(model, flipped(row, mask), source)
            normalize(model, source)

    entries = head_ref.shape[1]
    tile = max(size for size in range(16, 401, 16) if entries % size == 0)
    tokens = final.shape[1]

    def score(model, local_ids):
        with jax.named_scope("head"):
            head_loads[model].wait()

            def scan(index, state):
                peak, spread, picked = state
                start = pl.multiple_of(index * tile, tile)
                logits = lax.dot_general(
                    head[model, pl.ds(start, tile), :],
                    final[model],
                    (((1,), (1,)), ((), ())),
                    preferred_element_type=jnp.float32,
                )
                new_peak = jnp.maximum(peak, jnp.max(logits, axis=0, keepdims=True))
                spread = spread * jnp.exp(peak - new_peak) + jnp.sum(
                    jnp.exp(logits - new_peak), axis=0, keepdims=True
                )
                entry = lax.broadcasted_iota(jnp.int32, (tile, tokens), 0) + start
                picked = picked + jnp.sum(
                    jnp.where(entry == local_ids, logits, 0.0), axis=0, keepdims=True
                )
                return new_peak, spread, picked

            zero = jnp.zeros((1, tokens), jnp.float32)
            found = lax.fori_loop(0, entries // tile, scan, (zero - jnp.inf, zero, zero))
            for kind in range(3):
                for index in range(tokens // LANES):
                    stats[index, pl.ds(3 * model + kind, 1), :] = found[kind][
                        :, index * LANES : (index + 1) * LANES
                    ]

    counters = [iter(range(hidden_send.shape[1])) for _ in range(models)]
    state_load.wait()
    for model in range(models):
        mix(model)
        gated_norm(model)
    pass_weights()
    stats[...] = jnp.zeros_like(stats)
    for step in range(1, shards):
        other = lax.rem(me + step, shards)
        landing(targets_in.at[other], target_recv.at[other])
    tiles = [None] * (tokens // LANES)
    for source in range(columns):
        for line in range(outer):
            index = ((source * outer + line) * share) // LANES
            term = targets_in[line * columns + source, 0:1, :]
            tiles[index] = term if tiles[index] is None else tiles[index] + term
    local_ids = jnp.concatenate(tiles, axis=1) - me * entries
    for model in range(models):
        project(model)
        reduce(model)
    pass_line(0)
    pass_plane(0)
    for model in range(1, models):
        pass_line(model)
        collect(model - 1)
        score(model - 1, local_ids)
        pass_plane(model)
    collect(models - 1)
    score(models - 1, local_ids)

    with jax.named_scope("merge"):

        def tile_of(shard):
            return (((shard % columns) * outer + shard // columns) * share) // LANES

        for step in range(1, shards):
            other = lax.rem(me + step, shards)
            send(
                stats.at[tile_of(other)],
                stats_in.at[me],
                stats_send.at[step],
                stats_recv.at[me],
                (other, lane),
            )
        stats_in[me] = stats[tile_of(me)]
        for step in range(1, shards):
            other = lax.rem(me + step, shards)
            landing(stats_in.at[other], stats_recv.at[other])
        for model in range(models):
            peaks = stats_in[:, 3 * model, :]
            peak = jnp.max(peaks, axis=0, keepdims=True)
            spread = jnp.sum(
                stats_in[:, 3 * model + 1, :] * jnp.exp(peaks - peak), axis=0, keepdims=True
            )
            picked = jnp.sum(stats_in[:, 3 * model + 2, :], axis=0, keepdims=True)
            result_ref[model : model + 1, :] = picked - (peak + jnp.log(spread))
    for index in range(per_group):
        pl.when(lane * per_group + index != row)(lambda index=index: resid_copy(index).wait_send())
    for copy in pending:
        copy.wait_send()


def local(
    gate_in,
    mix_in,
    keys_in,
    step_in,
    resid_in,
    kernel_mix,
    kernel_keys,
    step_bias,
    decay_rate,
    skip_gain,
    norm_gain,
    final_gain,
    out_weight,
    head_weight,
    history_mix,
    history_keys,
    start_state,
    lengths,
    continued,
    targets,
    score_flag,
):
    groups = lax.axis_size("tp")
    shards = lax.axis_size("req")
    lane_index = lax.axis_index("tp")
    shard_index = lax.axis_index("req")
    outer, inner = split_shards(shards)
    columns = inner * CORES
    models, step_count, inner_part = gate_in.shape
    share = step_count // groups
    features = final_gain.shape[1]
    width = features // outer
    vocab_part = head_weight.shape[1]
    tokens = shards * share
    row, column = shard_index // columns, shard_index % columns
    weights = out_weight
    if out_weight.shape[2] % LANES:
        planes = [[z * columns + c for c in range(columns)] for z in range(outer)]
        weights = lax.all_gather(out_weight, "req", axis=2, tiled=True, axis_index_groups=planes)
    spot = ((column * outer + row) * share) % LANES
    own_targets = lax.dynamic_slice_in_dim(targets, lane_index * share, share, 0)
    target_tile = jnp.broadcast_to(
        lax.dynamic_update_slice_in_dim(jnp.zeros(LANES, jnp.int32), own_targets, spot, 0)[None, :],
        (8, LANES),
    )
    rows = models * step_count
    line_rows = outer * share
    sends = outer - 1 + outer * (inner - 1) + outer * inner
    dma = pltpu.SemaphoreType.DMA
    vmem = pl.BlockSpec(memory_space=pltpu.VMEM)
    smem = pl.BlockSpec(memory_space=pltpu.SMEM)
    anywhere = pl.BlockSpec(memory_space=pl.ANY)
    operands = (
        gate_in,
        mix_in,
        keys_in,
        step_in,
        kernel_mix,
        kernel_keys,
        step_bias,
        decay_rate,
        skip_gain,
        history_mix,
        history_keys,
        norm_gain,
        final_gain,
        resid_in,
        target_tile,
    )
    scores = pl.pallas_call(
        functools.partial(score_kernel, outer, inner, groups, len(operands)),
        out_shape=jax.ShapeDtypeStruct((models, LANES), jnp.float32),
        in_specs=[anywhere] * len(operands) + [smem] * 2 + [anywhere] * 3,
        out_specs=vmem,
        scratch_shapes=[pltpu.VMEM(operand.shape, operand.dtype) for operand in operands]
        + [
            dma((len(operands),)),
            pltpu.VMEM(start_state.shape, jnp.bfloat16),
            pltpu.VMEM((rows, inner_part), jnp.float32),
            pltpu.VMEM((outer, models, step_count, width), jnp.bfloat16),
            pltpu.VMEM((shards, 8, LANES), jnp.int32),
            pltpu.VMEM((models, inner_part, width), jnp.bfloat16),
            pltpu.VMEM((models, vocab_part, features), jnp.bfloat16),
            pltpu.VMEM((groups, models, step_count, LANES), jnp.float32),
            pltpu.VMEM((models, outer, step_count, inner_part), jnp.bfloat16),
            pltpu.VMEM((groups, models, outer, share, width), jnp.float32),
            pltpu.VMEM((groups, models, outer, share, width), jnp.float32),
            pltpu.VMEM((line_rows, width), jnp.float32),
            pltpu.VMEM((models, outer, columns, line_rows, width), jnp.bfloat16),
            pltpu.VMEM((models, tokens, features), jnp.bfloat16),
            pltpu.VMEM((tokens // LANES, 8, LANES), jnp.float32),
            pltpu.VMEM((shards, 8, LANES), jnp.float32),
            dma,
            dma((outer // groups,)),
            dma((outer,)),
            dma((shards,)),
            dma((shards,)),
            dma,
            dma((2 * inner,)),
            dma((columns,)),
            dma((models,)),
            dma((groups, models)),
            dma((groups, models)),
            dma((models, outer)),
            dma((models, outer)),
            dma((groups, models, outer)),
            dma((groups, models, outer)),
            dma((models, sends)),
            dma((models, outer, columns)),
            dma((shards,)),
            dma((shards,)),
        ],
        compiler_params=pltpu.CompilerParams(
            collective_id=0, has_side_effects=True, vmem_limit_bytes=50 * 1024 * 1024
        ),
    )(*operands, lengths, continued, start_state, weights, head_weight)
    own_scores = lax.dynamic_slice_in_dim(scores, spot, share, 1)
    scored_rows = lax.dynamic_slice_in_dim(score_flag, lane_index * share, share, 0)
    return own_scores * scored_rows.astype(jnp.float32)[None, :]


def solution(mesh):
    placed = (
        P(None, "req", "tp"),
        P(None, "req", "tp"),
        P(None, "req", None),
        P(None, "req", "tp"),
        P(None, "req", "tp"),
        P(None, None, "tp"),
        P(),
        P(None, "tp"),
        P(None, "tp"),
        P(None, "tp"),
        P(None, "tp"),
        P(),
        P(None, "tp", "req"),
        P(None, "req", None),
        P(None, "req", None, "tp"),
        P(None, "req", None, None),
        P(None, "req", "tp", None),
        P("req", None),
        P("req", None),
        P("req"),
        P("req"),
    )
    return jax.shard_map(
        local, mesh=mesh, in_specs=placed, out_specs=P(None, ("req", "tp")), check_vma=False
    )
```
